256 devices in a mesh: section: 16 (over y, z_lo, core), frame: 16 (over x, z_hi).
Axes of the slice: x: 4, y: 4, z: 8 (z_hi: 4, z_lo: 2; z = z_hi * 2 + z_lo), core: 2. Of those that a mesh axis runs over, the one named last changes fastest.
Arguments:
- gen_in: bfloat16 [64, 32, 128, 128], P(None, 'frame', 'section'), may hold values from -6 to 6
- w_gen_one: bfloat16 [9, 4096], replicated, may hold values from -0.25 to 0.25
- w_gen_rgb: bfloat16 [3, 64, 3, 3], replicated, may hold values from -0.25 to 0.25
- w_disc_one: bfloat16 [64, 3, 3, 3, 3], replicated, may hold values from -0.625 to 0.625
- w_disc_two: bfloat16 [27, 4096], replicated, may hold values from -0.15625 to 0.15625
- w_score: bfloat16 [64], replicated, may hold values from -0.75 to 0.75
- score_grad: float32 [32, 128, 128], P('frame', 'section'), may hold values from -6 to 6
Outputs:
- grad_in: bfloat16 [64, 32, 128, 128], P(None, 'frame', 'section')
- grad_gen_one: float32 [9, 4096], replicated
- grad_gen_rgb: float32 [3, 64, 3, 3], replicated
- grad_disc_one: float32 [64, 3, 3, 3, 3], replicated
- grad_disc_two: float32 [27, 4096], replicated
- grad_score: float32 [64], replicated
The draws below stay inside these ranges and needn't reach their ends.
All inputs are finite; a program needn't handle non-finite values.
Results may differ from the reference program's by a relative error of at most 0.019.
Values may be sent and summed in bfloat16 or wider, within the bound.
No kernel may reach another device: no remote copies, remote signals or barrier semaphores. Data moves between devices by JAX's collectives and lax.ppermute only.
A program may use at most 64 MiB of HBM per device.

```python
import jax
import jax.numpy as jnp
from jax import lax

C = 64
DH = 64
WID = 128
FRAMES = 32
H = 128


def block_scale(stream_key, dims, cuts, least, high):
    factor_of = 1.0
    for dim, blocks in cuts:
        steps = jax.random.uniform(jax.random.fold_in(jax.random.fold_in(stream_key, 6), dim), (blocks,), jnp.float32, least / len(cuts), high / len(cuts))
        factor_of = factor_of * jnp.repeat(jnp.exp(steps), dims[dim] // blocks).reshape((-1,) + (1,) * (len(dims) - 1 - dim))
    return factor_of


def scatter_about(own_key, dims, spread, most, split=(), dtype=jnp.bfloat16):
    factor_of = block_scale(own_key, dims, split, -0.22, 0.18) if split else 1.0
    drawn = jax.random.normal(own_key, dims, jnp.float32) * spread * factor_of
    return jnp.minimum(jnp.maximum(drawn, -most), most).astype(dtype)


def setup_inputs(seed: int = 0) -> dict:
    splits = jax.random.split(jax.random.key(seed), 8)
    return {
        "gen_in": scatter_about(splits[0], (C, FRAMES, H, WID), 1.0, 6.0, ((1, 16), (2, 16))),
        "w_gen_one": scatter_about(splits[1], (9, C * C), (9 * C) ** -0.5, 0.25),
        "w_gen_rgb": scatter_about(splits[2], (3, C, 3, 3), (9 * C) ** -0.5, 0.25),
        "w_disc_one": scatter_about(splits[3], (DH, 3, 3, 3, 3), 81 ** -0.5, 0.625),
        "w_disc_two": scatter_about(splits[4], (27, DH * DH), (27 * DH) ** -0.5, 0.15625),
        "w_score": scatter_about(splits[5], (DH,), DH ** -0.5, 0.75),
        "score_grad": scatter_about(splits[6], (FRAMES, H, WID), 1.0, 6.0, ((0, 16), (1, 16)), jnp.float32),
    }


def squash(z):
    return jnp.tanh(z)


def slope(a):
    value = a.astype(jnp.float32)
    return 1.0 - value * value


def plane_kernel(flat, outs, ins):
    return jnp.transpose(flat.reshape(3, 3, outs, ins), (2, 3, 0, 1))


def volume_kernel(flat, outs, ins):
    return jnp.transpose(flat.reshape(3, 3, 3, outs, ins), (3, 4, 0, 1, 2))


def plane_flat(kernel):
    return jnp.transpose(kernel, (2, 3, 0, 1)).reshape(9, -1)


def volume_flat(kernel):
    return jnp.transpose(kernel, (2, 3, 4, 0, 1)).reshape(27, -1)


def conv_plane(xp, w):
    return lax.conv_general_dilated(xp, w, (1, 1), "VALID", dimension_numbers=("CNHW", "OIHW", "CNHW"), preferred_element_type=jnp.float32)


def conv_volume(xp, w):
    return lax.conv_general_dilated(xp[None], w, (1, 1, 1), "VALID", dimension_numbers=("NCDHW", "OIDHW", "NCDHW"), preferred_element_type=jnp.float32)[0]


def back_plane(dyp, w):
    return conv_plane(dyp, jnp.swapaxes(jnp.flip(w, (2, 3)), 0, 1))


def back_volume(dyp, w):
    return conv_volume(dyp, jnp.swapaxes(jnp.flip(w, (2, 3, 4)), 0, 1))


def wgrad_plane(xp, dy):
    out = lax.conv_general_dilated(xp, dy, (1, 1), "VALID", dimension_numbers=("NCHW", "OIHW", "NCHW"), preferred_element_type=jnp.float32)
    return jnp.swapaxes(out, 0, 1)


def wgrad_volume(xp, dy):
    out = lax.conv_general_dilated(xp[:, None], dy[:, None], (1, 1, 1), "VALID", dimension_numbers=("NCDHW", "OIDHW", "NCDHW"), preferred_element_type=jnp.float32)
    return jnp.swapaxes(out, 0, 1)


def pad_plane(x):
    return jnp.pad(x, ((0, 0), (0, 0), (1, 1), (1, 1)))


def pad_volume(x):
    return jnp.pad(x, ((0, 0), (1, 1), (1, 1), (1, 1)))


def reference(gen_in, w_gen_one, w_gen_rgb, w_disc_one, w_disc_two, w_score, score_grad):
    factor = 1.0 / (FRAMES * H * WID) ** 0.5
    kernel_gen = plane_kernel(w_gen_one, C, C)
    kernel_two = volume_kernel(w_disc_two, DH, DH)
    gen_pad = pad_plane(gen_in)
    hidden = squash(conv_plane(gen_pad, kernel_gen)).astype(jnp.bfloat16)
    hidden_pad = pad_plane(hidden)
    colour = conv_plane(hidden_pad, w_gen_rgb).astype(jnp.bfloat16)
    colour_pad = pad_volume(colour)
    feat_one = squash(conv_volume(colour_pad, w_disc_one)).astype(jnp.bfloat16)
    feat_pad = pad_volume(feat_one)
    feat_two = squash(conv_volume(feat_pad, kernel_two)).astype(jnp.bfloat16)
    grad_score = jnp.einsum("cfhw,fhw->c", feat_two.astype(jnp.float32), score_grad) * factor
    dz_two = (w_score.astype(jnp.float32)[:, None, None, None] * score_grad[None] * slope(feat_two)).astype(jnp.bfloat16)
    grad_disc_two = volume_flat(wgrad_volume(feat_pad, dz_two)) * factor
    dz_one = (back_volume(pad_volume(dz_two), kernel_two) * slope(feat_one)).astype(jnp.bfloat16)
    grad_disc_one = wgrad_volume(colour_pad, dz_one) * factor
    d_colour = back_volume(pad_volume(dz_one), w_disc_one).astype(jnp.bfloat16)
    grad_gen_rgb = wgrad_plane(hidden_pad, d_colour) * factor
    dz_hidden = (back_plane(pad_plane(d_colour), w_gen_rgb) * slope(hidden)).astype(jnp.bfloat16)
    grad_gen_one = plane_flat(wgrad_plane(gen_pad, dz_hidden)) * factor
    grad_in = back_plane(pad_plane(dz_hidden), kernel_gen).astype(jnp.bfloat16)
    return (grad_in, grad_gen_one, grad_gen_rgb, grad_disc_one, grad_disc_two, grad_score)
```

```python
import jax
import jax.numpy as jnp
from jax import lax
from jax.experimental import pallas as pl
from jax.experimental.pallas import tpu as pltpu
from jax.sharding import PartitionSpec as P

BF = jnp.bfloat16
F32 = jnp.float32
C = 64
C3 = 3 * C
L = 128
BOTH = ("section", "frame")


def span(row, rows=1):
    return slice(row * L, (row + rows) * L)


def lanes():
    return lax.broadcasted_iota(jnp.int32, (1, L), 1)


def sides(value):
    at = lanes()
    left = jnp.where(at == 0, 0.0, pltpu.roll(value, 1, 1))
    right = jnp.where(at == L - 1, 0.0, pltpu.roll(value, L - 1, 1))
    return left, right


def put(ref, row, value):
    left, right = sides(value)
    ref[0:C, span(row)] = left.astype(BF)
    ref[C : 2 * C, span(row)] = value.astype(BF)
    ref[2 * C : C3, span(row)] = right.astype(BF)


def inside(index, size):
    return jnp.where(jnp.logical_and(index >= 0, index < size), 1.0, 0.0).astype(F32)


def product(out, weight, block, rows, step=4):
    for row in range(0, rows, step):
        part = span(row, min(step, rows - row))
        out[:, part] = jnp.dot(weight[...], block(part), preferred_element_type=F32)


def tap_rows(part, row, outs):
    return (
        part[0:outs, span(row)]
        + part[outs : 2 * outs, span(row + 1)]
        + part[2 * outs : 3 * outs, span(row + 2)]
    )


def along_lanes(a, b):
    return lax.dot_general(a, b, (((1,), (1,)), ((), ())), preferred_element_type=F32)


def three_rows(value):
    blank = jnp.zeros((value.shape[0], L), BF)
    return jnp.concatenate(
        [
            jnp.concatenate([value, blank, blank], axis=1),
            jnp.concatenate([blank, value, blank], axis=1),
            jnp.concatenate([blank, blank, value], axis=1),
        ],
        axis=0,
    )


def gen_kernel(up, mid, down, w_gen, w_rgb, edge, hid, gen, gs, hs, part, part_rgb):
    section = lax.axis_index("section")
    rows_all = 8 * lax.axis_size("section")
    base = section * 8

    for f in range(2):
        for row in range(24):
            source = (up, mid, down)[row // 8]
            keep = inside(base + row - 8, rows_all)
            value = source[0:C, span(f * 8 + row % 8)].astype(F32) * keep
            put(gs, row, value)
        product(part, w_gen, lambda s: gs[:, s], 24)
        gen[f] = gs[:, span(7, 10)]
        for row in range(22):
            keep = inside(base + row - 7, rows_all)
            put(hs, row, jnp.tanh(tap_rows(part, row, C)) * keep)
        product(part_rgb, w_rgb, lambda s: hs[:, s], 22)
        hid[f] = hs[:, span(6, 10)]
        for row in range(20):
            at = row + 2
            source = (up, mid, down)[at // 8]
            score = source[C : C + 16, span(f * 8 + at % 8)].astype(F32)[0:8]
            keep = inside(base + row - 6, rows_all)
            value = (tap_rows(part_rgb, row, 8) + score) * keep
            edge[:, span(f * 20 + row)] = value.astype(BF)


def disc_kernel(
    e0, e1, e2, e3, e4, w_one, w_two, w_two_back, w_one_back, w_rgb_back, w_gen_back, w_score, hid, gen,
    grad_in, pack,
    es, cs, sg, fs, ds, zs, dcs, hzs, part, part_one, part_col, acc_two, acc_gen, acc_one, acc_rgb, acc_score,
):
    section = lax.axis_index("section")
    frame = lax.axis_index("frame")
    rows_all = 8 * lax.axis_size("section")
    frames_all = 2 * lax.axis_size("frame")
    base = section * 8
    first = frame * 2
    sub = lax.broadcasted_iota(jnp.int32, (8, L), 0)

    for k, e in enumerate((e0, e1, e2, e3, e4)):
        for j in range(2):
            es[2 * k + j] = e[:, span(20 * j, 20)].astype(F32)

    def colour_step(e, carry):
        keep = inside(first + e - 4, frames_all)
        for row in range(20):
            value = es[e, :, span(row)] * keep
            sg[e, row : row + 1, :] = value[3:4] + value[4:5]
            value = jnp.where(sub < 3, value, 0.0)
            left, right = sides(value)
            block = jnp.concatenate([left + pltpu.roll(value, 4, 0), right], axis=0).astype(BF)
            for dr in range(3):
                if 0 <= row - dr < 18:
                    cs[e, dr * 16 : (dr + 1) * 16, span(row - dr)] = block
        return carry

    lax.fori_loop(0, 10, colour_step, 0)

    def feat_step(p, carry):
        product(part_one, w_one, lambda s: cs[pl.ds(2 * p, 4), :, s].reshape(192, -1), 18)
        for j in range(2):
            u = 2 * p + j
            keep_frame = inside(first + u - 3, frames_all)
            for row in range(18):
                keep = inside(base + row - 5, rows_all) * keep_frame
                put(fs.at[u], row, jnp.tanh(part_one[j * C : (j + 1) * C, span(row)]) * keep)
        return carry

    lax.fori_loop(0, 4, feat_step, 0)

    acc_score[...] = jnp.zeros_like(acc_score)

    def score_step(g, carry):
        product(part, w_two, lambda s: fs[pl.ds(g, 3), :, s].reshape(3 * C3, -1), 18)
        own = inside(g - 2, 2)
        for row in range(16):
            value = jnp.tanh(tap_rows(part, row, C)).astype(BF).astype(F32)
            score = sg[g + 2, row + 2 : row + 3, :]
            if 4 <= row < 12:
                acc_score[...] += value * (score * own)
            put(ds.at[g], row, w_score[...] * score * (1.0 - value * value))
        return carry

    lax.fori_loop(0, 6, score_step, 0)

    def back_step(h, carry):
        product(part, w_two_back, lambda s: ds[pl.ds(h, 3), :, s].reshape(3 * C3, -1), 16)
        keep_frame = inside(first + h - 1, frames_all)
        for row in range(14):
            keep = inside(base + row - 3, rows_all) * keep_frame
            value = fs[h + 2, C : 2 * C, span(row + 2)].astype(F32)
            put(zs.at[h], row, tap_rows(part, row, C) * ((1.0 - value * value) * keep))
        return carry

    lax.fori_loop(0, 4, back_step, 0)

    for f in range(2):
        feat = fs[f + 2 : f + 5, :, span(4, 10)].reshape(3 * C3, 10 * L)
        grad = along_lanes(three_rows(ds[f + 2, C : 2 * C, span(4, 8)]), feat)
        acc_two[...] = grad if f == 0 else acc_two[...] + grad
        colours = cs[f + 3 : f + 6, :, span(5, 8)].reshape(144, 8 * L)
        grad = along_lanes(colours, zs[f + 1, C : 2 * C, span(3, 8)])
        acc_one[...] = grad if f == 0 else acc_one[...] + grad

        product(part_col, w_one_back, lambda s: zs[f : f + 3, :, s].reshape(3 * C3, -1), 14)
        colour_rows = []
        for row in range(12):
            keep = inside(base + row - 2, rows_all)
            value = (tap_rows(part_col, row, 8) * keep).astype(BF).astype(F32)
            colour_rows.append(value)
            left, right = sides(value)
            block = jnp.concatenate([left + pltpu.roll(value, 4, 0), right], axis=0)
            dcs[:, span(row)] = block.astype(BF)
        own = jnp.concatenate(colour_rows[2:10], axis=1)
        blank = jnp.zeros((8, L), F32)
        own3 = jnp.concatenate(
            [
                jnp.concatenate([own, blank, blank], axis=1),
                jnp.concatenate([blank, own, blank], axis=1),
                jnp.concatenate([blank, blank, own], axis=1),
                jnp.zeros((8, 10 * L), F32),
            ],
            axis=0,
        ).astype(BF)
        grad = along_lanes(hid[f], own3)
        acc_rgb[...] = grad if f == 0 else acc_rgb[...] + grad

        product(part, w_rgb_back, lambda s: dcs[:, s], 12)
        for row in range(10):
            keep = inside(base + row - 1, rows_all)
            value = hid[f, C : 2 * C, span(row)].astype(F32)
            put(hzs, row, tap_rows(part, row, C) * ((1.0 - value * value) * keep))
        grad = along_lanes(three_rows(hzs[C : 2 * C, span(1, 8)]), gen[f])
        acc_gen[...] = grad if f == 0 else acc_gen[...] + grad
        product(part, w_gen_back, lambda s: hzs[:, s], 10)
        for row in range(8):
            grad_in[:, span(f * 8 + row)] = tap_rows(part, row, C).astype(BF)

    score = jnp.sum(acc_score[...], axis=1, keepdims=True)
    tail = jnp.concatenate(
        [jnp.broadcast_to(score, (C, 32)), jnp.zeros((C3 - C, 32), F32)], axis=0
    )
    ones = jnp.concatenate([acc_one[...], jnp.zeros((C3 - 144, C), F32)], axis=0)
    whole = jnp.concatenate([acc_two[...], acc_gen[...], ones, acc_rgb[...], tail], axis=1)
    for k in range(8):
        pack[k] = whole[24 * k : 24 * (k + 1)].astype(BF)


def call(kernel, outs, scratch, name):
    return pl.pallas_call(
        kernel,
        out_shape=outs,
        scratch_shapes=scratch,
        compiler_params=pltpu.CompilerParams(vmem_limit_bytes=50 << 20),
        name=name,
    )


def cyclic(value, axis, step):
    size = lax.axis_size(axis)
    return lax.ppermute(value, axis, [(i, (i + step) % size) for i in range(size)])


def swapped(value, axis, mask):
    return lax.ppermute(value, axis, [(i, i ^ mask) for i in range(lax.axis_size(axis))])


def pick(value, at):
    return lax.dynamic_index_in_dim(value, at, 0, keepdims=False)


def plus(values):
    total = values[0].astype(F32)
    for value in values[1:]:
        total = total + value.astype(F32)
    return total.astype(BF)


def all_sum4(value, axis, low):
    one, two, three = (swapped(value, axis, m * low).astype(F32) for m in (1, 2, 3))
    return ((value.astype(F32) + one) + (two + three)).astype(BF)


def gathered(value, axis, low, count, me):
    parts = jnp.stack([value] + [swapped(value, axis, m * low) for m in range(1, count)])
    return jnp.stack([pick(parts, me ^ k) for k in range(count)])


def summed(value):
    section = lax.axis_index("section")
    core = section & 1
    y = (section >> 2) & 3
    halves = value.reshape((2, 4) + value.shape[1:])
    mine = plus([pick(halves, core), swapped(pick(halves, 1 - core), "section", 1)])
    own = plus([pick(mine, y)] + [swapped(pick(mine, y ^ m), "section", 4 * m) for m in (1, 2, 3)])
    own = all_sum4(own, "frame", 4)
    own = plus([own, swapped(own, "section", 2)])
    own = all_sum4(own, "frame", 1)
    mine = gathered(own, "section", 4, 4, y)
    both = gathered(mine, "section", 1, 2, core)
    return both.reshape(value.shape)


def local(gen_in, w_gen_one, w_gen_rgb, w_disc_one, w_disc_two, w_score, score_grad):
    cells = 2048 * lax.axis_size("frame") * lax.axis_size("section")
    factor = 1.0 / cells**0.5

    gen = w_gen_one.reshape(3, 3, C, C)
    w_gen = jnp.transpose(gen, (0, 2, 1, 3)).reshape(C3, C3)
    w_gen_back = jnp.transpose(jnp.flip(gen, (0, 1)), (0, 3, 1, 2)).reshape(C3, C3)
    rgb = jnp.pad(jnp.transpose(w_gen_rgb, (2, 0, 3, 1)), ((0, 0), (0, 5), (0, 0), (0, 0)))
    w_rgb = rgb.reshape(24, C3)
    rgb_back = jnp.transpose(jnp.flip(w_gen_rgb, (2, 3)), (2, 1, 3, 0))
    w_rgb_back = jnp.pad(rgb_back, ((0, 0), (0, 0), (0, 1), (0, 1))).reshape(C3, 16)
    two = w_disc_two.reshape(3, 3, 3, C, C)
    w_two = jnp.transpose(two, (1, 3, 0, 2, 4)).reshape(C3, 3 * C3)
    w_two_back = jnp.transpose(jnp.flip(two, (0, 1, 2)), (1, 4, 0, 2, 3)).reshape(C3, 3 * C3)
    one = jnp.transpose(w_disc_one, (0, 2, 3, 4, 1))
    one = jnp.pad(one, ((0, 0), (0, 0), (0, 0), (0, 1), (0, 1))).reshape(C, 144)
    w_one = jnp.concatenate(
        [jnp.pad(one, ((0, 0), (0, 48))), jnp.pad(one, ((0, 0), (48, 0)))], axis=0
    )
    one_back = jnp.transpose(jnp.flip(w_disc_one, (2, 3, 4)), (3, 1, 2, 4, 0))
    w_one_back = jnp.pad(one_back, ((0, 0), (0, 5), (0, 0), (0, 0), (0, 0))).reshape(24, 3 * C3)
    score_w = jnp.broadcast_to(w_score.astype(F32)[:, None], (C, L))

    score = score_grad.reshape(1, 2048)
    high = score.astype(BF)
    low = (score - high.astype(F32)).astype(BF)
    mid = jnp.concatenate(
        [gen_in.reshape(C, 2048), jnp.zeros((3, 2048), BF), high, low, jnp.zeros((11, 2048), BF)],
        axis=0,
    )
    up = cyclic(mid, "section", 1)
    down = cyclic(mid, "section", -1)

    edge, hid, gen_pad = call(
        gen_kernel,
        (
            jax.ShapeDtypeStruct((8, 40 * L), BF),
            jax.ShapeDtypeStruct((2, C3, 10 * L), BF),
            jax.ShapeDtypeStruct((2, C3, 10 * L), BF),
        ),
        [
            pltpu.VMEM((C3, 24 * L), BF),
            pltpu.VMEM((C3, 22 * L), BF),
            pltpu.VMEM((C3, 24 * L), F32),
            pltpu.VMEM((24, 22 * L), F32),
        ],
        "generator",
    )(up, mid, down, w_gen, w_rgb)

    edges = [cyclic(edge, "frame", s) for s in (2, -2, 1, -1)]
    grad_in, pack = call(
        disc_kernel,
        (jax.ShapeDtypeStruct((C, 2048), BF), jax.ShapeDtypeStruct((8, 24, 896), BF)),
        [
            pltpu.VMEM((10, 8, 20 * L), F32),
            pltpu.VMEM((10, 48, 18 * L), BF),
            pltpu.VMEM((10, 24, L), F32),
            pltpu.VMEM((8, C3, 18 * L), BF),
            pltpu.VMEM((6, C3, 16 * L), BF),
            pltpu.VMEM((4, C3, 14 * L), BF),
            pltpu.VMEM((16, 12 * L), BF),
            pltpu.VMEM((C3, 10 * L), BF),
            pltpu.VMEM((C3, 18 * L), F32),
            pltpu.VMEM((2 * C, 18 * L), F32),
            pltpu.VMEM((24, 14 * L), F32),
            pltpu.VMEM((C3, 3 * C3), F32),
            pltpu.VMEM((C3, C3), F32),
            pltpu.VMEM((144, C), F32),
            pltpu.VMEM((C3, 32), F32),
            pltpu.VMEM((C, L), F32),
        ],
        "discriminator",
    )(
        edges[0], edges[2], edge, edges[3], edges[1],
        w_one, w_two, w_two_back, w_one_back, w_rgb_back, w_gen_back, score_w, hid, gen_pad,
    )

    total = summed(pack).reshape(C3, 896).astype(F32) * factor
    disc_two = jnp.transpose(total[:, : 3 * C3].reshape(3, C, 3, 3, C), (2, 0, 3, 1, 4)).reshape(27, C * C)
    gen_one = jnp.transpose(total[:, 576:768].reshape(3, C, 3, C), (0, 2, 1, 3)).reshape(9, C * C)
    disc_one = total[:144, 768:832].reshape(3, 3, 4, 4, C)[:, :, :3, :3]
    disc_one = jnp.transpose(disc_one, (4, 3, 0, 1, 2))
    gen_rgb = total[:, 832:856].reshape(3, C, 3, 8)[..., :3]
    gen_rgb = jnp.transpose(gen_rgb, (3, 1, 2, 0))
    disc_score = total[:C, 864]
    return (grad_in.reshape(gen_in.shape), gen_one, gen_rgb, disc_one, disc_two, disc_score)


def solution(mesh):
    in_specs = (
        P(None, "frame", "section", None),
        P(),
        P(),
        P(),
        P(),
        P(),
        P("frame", "section", None),
    )
    out_specs = (P(None, "frame", "section", None), P(), P(), P(), P(), P())
    return jax.shard_map(local, mesh=mesh, in_specs=in_specs, out_specs=out_specs, check_vma=False)
```

```python
import functools

import jax
import jax.numpy as jnp
from jax import lax
from jax.experimental import pallas as pl
from jax.experimental.pallas import tpu as pltpu
from jax.sharding import PartitionSpec as P

BF = jnp.bfloat16
F32 = jnp.float32
C = 64
C3 = 3 * C
L = 128
BOTH = ("section", "frame")


def span(row, rows=1):
    return slice(row * L, (row + rows) * L)


def lanes():
    return lax.broadcasted_iota(jnp.int32, (1, L), 1)


def sides(value):
    at = lanes()
    left = jnp.where(at == 0, 0.0, pltpu.roll(value, 1, 1))
    right = jnp.where(at == L - 1, 0.0, pltpu.roll(value, L - 1, 1))
    return left, right


def put(ref, row, value):
    left, right = sides(value)
    ref[0:C, span(row)] = left.astype(BF)
    ref[C : 2 * C, span(row)] = value.astype(BF)
    ref[2 * C : C3, span(row)] = right.astype(BF)


def inside(index, size):
    return jnp.where(jnp.logical_and(index >= 0, index < size), 1.0, 0.0).astype(F32)


def staged(out, weight, block, rows, outs, lag, finish, step=2):
    done = 0
    for row in range(0, rows, step):
        part = span(row, min(step, rows - row))
        out[:, part] = jnp.dot(weight[...], block(part), preferred_element_type=F32)
        while done < min(row - lag, outs):
            finish(done)
            done += 1
    for row in range(done, outs):
        finish(row)


def tap_rows(part, row, outs):
    return (
        part[0:outs, span(row)]
        + part[outs : 2 * outs, span(row + 1)]
        + part[2 * outs : 3 * outs, span(row + 2)]
    )


def along_lanes(a, b):
    return lax.dot_general(a, b, (((1,), (1,)), ((), ())), preferred_element_type=F32)


def three_rows(value):
    blank = jnp.zeros((value.shape[0], L), BF)
    return jnp.concatenate(
        [
            jnp.concatenate([value, blank, blank], axis=1),
            jnp.concatenate([blank, value, blank], axis=1),
            jnp.concatenate([blank, blank, value], axis=1),
        ],
        axis=0,
    )


def pack_kernel(features, scores, mid, wide):
    wide[...] = features[...].astype(F32)
    sub = lax.broadcasted_iota(jnp.int32, (16, L), 0)
    for k in range(16):
        mid[0:C, span(k)] = wide[pl.ds(k, C, stride=16), :].astype(BF)
        score = scores[k : k + 1, :]
        high = score.astype(BF).astype(F32)
        both = jnp.where(sub == 0, high, jnp.where(sub == 1, score - high, 0.0))
        mid[C : C + 16, span(k)] = both.astype(BF)


def weight_kernel(
    flat_two, flat_gen, two, two_back, gen, gen_back, taps, blocks,
):
    for j in range(32):
        taps[pl.ds(j, 27, stride=32), :] = flat_two[:, span(j)].astype(F32)
        taps[pl.ds(27 * 32 + j, 9, stride=32), :] = flat_gen[:, span(j)].astype(F32)
    for dr in range(3):
        for b in range(6):
            pair = []
            for tap in (2 * b, 2 * b + 1):
                at = (tap // 3) * 9 + dr * 3 + tap % 3 if tap < 9 else 27 + dr * 3 + tap - 9
                pair.append(taps[32 * at : 32 * at + 32, :])
            for odd in range(2):
                half = slice(C * odd, C * odd + C)
                blocks[b, pl.ds(C * dr + odd, 32, stride=2), :] = jnp.concatenate(
                    [pair[0][:, half], pair[1][:, half]], axis=1
                )
    for dr in range(3):
        rows = slice(C * dr, C * dr + C)
        mirror = slice(C * (2 - dr), C * (2 - dr) + C)
        ahead = [blocks[b, rows, :] for b in range(6)]
        ahead = [block[:, C * h : C * h + C] for block in ahead for h in range(2)]
        two[rows, :] = jnp.concatenate(ahead[:9], axis=1).astype(BF)
        gen[rows, :] = jnp.concatenate(ahead[9:], axis=1).astype(BF)
        back = [jnp.transpose(blocks[b, rows, :]) for b in range(6)]
        back = [block[C * h : C * h + C, :] for block in back for h in range(2)]
        two_back[mirror, :] = jnp.concatenate(back[8::-1], axis=1).astype(BF)
        gen_back[mirror, :] = jnp.concatenate(back[:8:-1], axis=1).astype(BF)


def gen_kernel(up, mid, down, w_gen, w_rgb, near, far, hid, gen, gs, hs, part, part_rgb, rows):
    section = lax.axis_index("section")
    rows_all = 8 * lax.axis_size("section")
    base = section * 8

    rows[...] = jnp.zeros_like(rows)
    for f in range(2):
        for row in range(24):
            source = (up, mid, down)[row // 8]
            keep = inside(base + row - 8, rows_all)
            value = source[0:C, span(f * 8 + row % 8)].astype(F32) * keep
            put(gs, row, value)
        def hidden_row(row):
            keep = inside(base + row - 7, rows_all)
            put(hs, row, jnp.tanh(tap_rows(part, row, C)) * keep)

        def colour_row(row):
            keep = inside(base + row - 6, rows_all)
            rows[3 * row : 3 * row + 3, span(f)] = (tap_rows(part_rgb, row, 8) * keep)[0:3]

        staged(part, w_gen, lambda s: gs[:, s], 24, 22, 2, hidden_row)
        gen[f] = gs[:, span(7, 10)]
        staged(part_rgb, w_rgb, lambda s: hs[:, s], 22, 20, 2, colour_row)
        hid[f] = hs[:, span(6, 10)]
        for row in range(16):
            at = row + 4
            source = (up, mid, down)[at // 8]
            keep = inside(base + row - 4, rows_all)
            score = source[C : C + 16, span(f * 8 + at % 8)].astype(F32) * keep
            rows[C + row : C + row + 1, span(f)] = score[0:1]
            rows[C + 16 + row : C + 17 + row, span(f)] = score[1:2]
    near[...] = rows[...].astype(BF)
    far[...] = rows[0:C, :].astype(BF)


def disc_kernel(
    far_a, far_b, near_a, near_b, home, w_one, w_two, w_two_back, w_one_back, w_rgb_back, w_gen_back, w_score, hid, gen,
    grad_in, pack,
    es, cs, sg, fs, ds, zs, dcs, hzs, part, part_one, part_col, acc, acc_one, acc_rgb, acc_score,
):
    section = lax.axis_index("section")
    frame = lax.axis_index("frame")
    rows_all = 8 * lax.axis_size("section")
    frames_all = 2 * lax.axis_size("frame")
    base = section * 8
    first = frame * 2
    sub = lax.broadcasted_iota(jnp.int32, (8, L), 0)

    turn_far, turn_near = (frame >> 1) & 1, frame & 1
    blocks = (
        (far_a, jnp.where(turn_far == 0, 8, 0), C),
        (far_b, jnp.where(turn_far == 0, 0, 8), C),
        (near_a, jnp.where(turn_near == 0, 6, 2), C + 32),
        (near_b, jnp.where(turn_near == 0, 2, 6), C + 32),
        (home, 4, C + 32),
    )
    es[...] = jnp.zeros_like(es)
    for block, at, size in blocks:
        for j in range(2):
            es[at + j, 0:size, :] = block[:, span(j)].astype(F32)

    def colour_step(e, carry):
        keep = inside(first + e - 4, frames_all)
        sg[e] = (es[e, C : C + 16, :] + es[e, C + 16 : C + 32, :]) * keep
        for row in range(20):
            value = jnp.where(sub < 3, es[e, 3 * row : 3 * row + 8, :] * keep, 0.0)
            left, right = sides(value)
            block = jnp.concatenate([left + pltpu.roll(value, 4, 0), right], axis=0).astype(BF)
            for dr in range(3):
                if 0 <= row - dr < 18:
                    cs[e, dr * 16 : (dr + 1) * 16, span(row - dr)] = block
        return carry

    lax.fori_loop(0, 10, colour_step, 0)

    def feat_step(p, carry):
        def feat_row(row):
            keep_row = inside(base + row - 5, rows_all)
            for j in range(2):
                keep = keep_row * inside(first + 2 * p + j - 3, frames_all)
                put(fs.at[2 * p + j], row, jnp.tanh(part_one[j * C : (j + 1) * C, span(row)]) * keep)

        staged(part_one, w_one, lambda s: cs[pl.ds(2 * p, 4), :, s].reshape(192, -1), 18, 18, 0, feat_row)
        return carry

    lax.fori_loop(0, 4, feat_step, 0)

    acc_score[...] = jnp.zeros_like(acc_score)

    def score_step(g, carry):
        own = inside(g - 2, 2)

        def score_row(row):
            value = jnp.tanh(tap_rows(part, row, C)).astype(BF).astype(F32)
            score = sg[g + 2, row : row + 1, :]
            if 4 <= row < 12:
                acc_score[...] += value * (score * own)
            put(ds.at[g], row, w_score[...] * score * (1.0 - value * value))

        staged(part, w_two, lambda s: fs[pl.ds(g, 3), :, s].reshape(3 * C3, -1), 18, 16, 2, score_row)
        return carry

    lax.fori_loop(0, 6, score_step, 0)

    def back_step(h, carry):
        keep_frame = inside(first + h - 1, frames_all)

        def back_row(row):
            keep = inside(base + row - 3, rows_all) * keep_frame
            value = fs[h + 2, C : 2 * C, span(row + 2)].astype(F32)
            put(zs.at[h], row, tap_rows(part, row, C) * ((1.0 - value * value) * keep))

        staged(part, w_two_back, lambda s: ds[pl.ds(h, 3), :, s].reshape(3 * C3, -1), 16, 14, 2, back_row)
        return carry

    lax.fori_loop(0, 4, back_step, 0)

    for f in range(2):
        feat = fs[f + 2 : f + 5, :, span(4, 10)].reshape(3 * C3, 10 * L)
        grad = along_lanes(three_rows(ds[f + 2, C : 2 * C, span(4, 8)]), feat)
        acc[:, : 3 * C3] = grad if f == 0 else acc[:, : 3 * C3] + grad
        colours = cs[f + 3 : f + 6, :, span(5, 8)].reshape(144, 8 * L)
        grad = along_lanes(colours, zs[f + 1, C : 2 * C, span(3, 8)])
        acc_one[...] = grad if f == 0 else acc_one[...] + grad

        colour_rows = []

        def colour_row(row):
            keep = inside(base + row - 2, rows_all)
            value = (tap_rows(part_col, row, 8) * keep).astype(BF).astype(F32)
            colour_rows.append(value)
            left, right = sides(value)
            block = jnp.concatenate([left + pltpu.roll(value, 4, 0), right], axis=0)
            dcs[:, span(row)] = block.astype(BF)

        staged(part_col, w_one_back, lambda s: zs[f : f + 3, :, s].reshape(3 * C3, -1), 14, 12, 2, colour_row)
        own = jnp.concatenate(colour_rows[2:10], axis=1)
        blank = jnp.zeros((8, L), F32)
        own3 = jnp.concatenate(
            [
                jnp.concatenate([own, blank, blank], axis=1),
                jnp.concatenate([blank, own, blank], axis=1),
                jnp.concatenate([blank, blank, own], axis=1),
                jnp.zeros((8, 10 * L), F32),
            ],
            axis=0,
        ).astype(BF)
        grad = along_lanes(own3, hid[f])
        acc_rgb[...] = grad if f == 0 else acc_rgb[...] + grad

        def hidden_row(row):
            keep = inside(base + row - 1, rows_all)
            value = hid[f, C : 2 * C, span(row)].astype(F32)
            put(hzs, row, tap_rows(part, row, C) * ((1.0 - value * value) * keep))

        def input_row(row):
            grad_in[:, span(f * 8 + row)] = tap_rows(part, row, C).astype(BF)

        staged(part, w_rgb_back, lambda s: dcs[:, s], 12, 10, 2, hidden_row)
        grad = along_lanes(three_rows(hzs[C : 2 * C, span(1, 8)]), gen[f])
        acc[:, 3 * C3 :] = grad if f == 0 else acc[:, 3 * C3 :] + grad
        staged(part, w_gen_back, lambda s: hzs[:, s], 10, 8, 2, input_row)

    score = jnp.sum(jnp.transpose(acc_score[...]), axis=0, keepdims=True)
    ones = jnp.concatenate([acc_one[...], jnp.zeros((C3 - 144, C), F32)], axis=0)
    colours = [acc_rgb[0:24, C * k : C * k + C] for k in range(3)]
    colours = jnp.concatenate(colours + [score, jnp.zeros((C3 - 73, C), F32)], axis=0)
    tail = jnp.concatenate([ones, colours], axis=1)
    for k in range(8):
        block = [acc[C * dr + 8 * k : C * dr + 8 * k + 8, :] for dr in range(3)]
        whole = jnp.concatenate([jnp.concatenate(block, axis=0), tail[24 * k : 24 * k + 24]], axis=1)
        pack[k] = whole.astype(BF)


def finish_kernel(factor, own, three, two, one, other, gen_one, gen_rgb, disc_one, disc_two, disc_score, total, taps):
    section = lax.axis_index("section")
    core, y = section & 1, (section >> 2) & 3
    for at, (k, block) in enumerate(((0, own), (3, three), (2, two), (1, one))):
        rows = pl.ds(pl.multiple_of((core * 4 + (y ^ k)) * 24, 8), 24)
        others = pl.ds(pl.multiple_of(((1 - core) * 4 + (y ^ k)) * 24, 8), 24)
        for b in range(7):
            total[b, rows, :] = block[:, span(b)].astype(F32) * factor
            total[b, others, :] = other[at, :, span(b)].astype(F32) * factor
    for c in range(3):
        for dr in range(3):
            for df in range(3):
                disc_one[c, df, dr] = total[6, pl.ds(48 * df + 16 * dr + c, 3, stride=4), :][:, 0:C]
            for dw in range(3):
                at = 24 * dw + 8 * dr + c
                gen_rgb[c, dr, dw : dw + 1, :] = total[6, at : at + 1, :][:, C:]
    disc_score[...] = total[6, 72:73, :][:, C:]
    for dr in range(3):
        for b in range(6):
            for pair in range(4):
                first, second = (
                    total[b, pl.ds(8 * dr + 2 * pair + odd, 8, stride=24), :] for odd in range(2)
                )
                for h in range(2):
                    half = slice(C * h, C * h + C)
                    tap = 2 * b + h
                    at = (tap // 3) * 9 + dr * 3 + tap % 3 if tap < 9 else 27 + dr * 3 + tap - 9
                    taps[pl.ds(32 * at + pair, 8, stride=4), :] = jnp.concatenate(
                        [first[:, half], second[:, half]], axis=1
                    )
    for j in range(32):
        disc_two[:, span(j)] = taps[pl.ds(j, 27, stride=32), :]
        gen_one[:, span(j)] = taps[pl.ds(27 * 32 + j, 9, stride=32), :]


def call(kernel, outs, scratch, name):
    return pl.pallas_call(
        kernel,
        out_shape=outs,
        scratch_shapes=scratch,
        compiler_params=pltpu.CompilerParams(vmem_limit_bytes=50 << 20),
        name=name,
    )


def cyclic(value, axis, step):
    size = lax.axis_size(axis)
    return lax.ppermute(value, axis, [(i, (i + step) % size) for i in range(size)])


def swapped(value, axis, mask):
    return lax.ppermute(value, axis, [(i, i ^ mask) for i in range(lax.axis_size(axis))])


def neighbours(value, axis, step):
    size = lax.axis_size(axis)
    found = []
    for turn in range(2):
        pairs = [(i, (i + step) % size) for i in range(size) if (i // step) % 2 == turn]
        found.append(lax.ppermute(value, axis, pairs + [(j, i) for i, j in pairs]))
    return found


def pick(value, at):
    return lax.dynamic_index_in_dim(value, at, 0, keepdims=False)


def plus(values):
    total = values[0].astype(F32)
    for value in values[1:]:
        total = total + value.astype(F32)
    return total.astype(BF)


def all_sum4(value, axis, low):
    three, two, one = (swapped(value, axis, m * low).astype(F32) for m in (3, 2, 1))
    return ((three + two) + (one + value.astype(F32))).astype(BF)


def summed(value):
    section = lax.axis_index("section")
    core, y = section & 1, (section >> 2) & 3
    halves = value.reshape((2, 4) + value.shape[1:])
    mine = plus([pick(halves, core), swapped(pick(halves, 1 - core), "section", 1)])
    own = plus([pick(mine, y)] + [swapped(pick(mine, y ^ m), "section", 4 * m) for m in (1, 3, 2)])
    own = all_sum4(own, "frame", 4)
    own = plus([own, swapped(own, "section", 2)])
    own = all_sum4(own, "frame", 1)
    three, two, one = (swapped(own, "section", 4 * m) for m in (3, 2, 1))
    blocks = [own, three, two, one]
    return blocks + [swapped(jnp.stack(blocks), "section", 1)]


def local(gen_in, w_gen_one, w_gen_rgb, w_disc_one, w_disc_two, w_score, score_grad):
    cells = 2048 * lax.axis_size("frame") * lax.axis_size("section")
    factor = 1.0 / cells**0.5

    rgb = jnp.pad(jnp.transpose(w_gen_rgb, (2, 0, 3, 1)), ((0, 0), (0, 5), (0, 0), (0, 0)))
    w_rgb = rgb.reshape(24, C3)
    rgb_back = jnp.transpose(jnp.flip(w_gen_rgb, (2, 3)), (2, 1, 3, 0))
    w_rgb_back = jnp.pad(rgb_back, ((0, 0), (0, 0), (0, 1), (0, 1))).reshape(C3, 16)
    one = jnp.transpose(w_disc_one, (0, 2, 3, 4, 1))
    one = jnp.pad(one, ((0, 0), (0, 0), (0, 0), (0, 1), (0, 1))).reshape(C, 144)
    w_one = jnp.concatenate(
        [jnp.pad(one, ((0, 0), (0, 48))), jnp.pad(one, ((0, 0), (48, 0)))], axis=0
    )
    one_back = jnp.transpose(jnp.flip(w_disc_one, (2, 3, 4)), (3, 1, 2, 4, 0))
    w_one_back = jnp.pad(one_back, ((0, 0), (0, 5), (0, 0), (0, 0), (0, 0))).reshape(24, 3 * C3)
    w_two, w_two_back, w_gen, w_gen_back = call(
        weight_kernel,
        (
            jax.ShapeDtypeStruct((C3, 3 * C3), BF),
            jax.ShapeDtypeStruct((C3, 3 * C3), BF),
            jax.ShapeDtypeStruct((C3, C3), BF),
            jax.ShapeDtypeStruct((C3, C3), BF),
        ),
        [pltpu.VMEM((36 * 32, L), F32), pltpu.VMEM((6, C3, L), F32)],
        "weights",
    )(w_disc_two, w_gen_one)
    score_w = jnp.broadcast_to(w_score.astype(F32)[:, None], (C, L))

    mid = call(
        pack_kernel,
        jax.ShapeDtypeStruct((C + 16, 2048), BF),
        [pltpu.VMEM((16 * C, L), F32)],
        "pack",
    )(gen_in.reshape(16 * C, L), score_grad.reshape(16, L))
    up = cyclic(mid, "section", 1)
    down = cyclic(mid, "section", -1)

    near, far, hid, gen_pad = call(
        gen_kernel,
        (
            jax.ShapeDtypeStruct((C + 32, 2 * L), BF),
            jax.ShapeDtypeStruct((C, 2 * L), BF),
            jax.ShapeDtypeStruct((2, C3, 10 * L), BF),
            jax.ShapeDtypeStruct((2, C3, 10 * L), BF),
        ),
        [
            pltpu.VMEM((C3, 24 * L), BF),
            pltpu.VMEM((C3, 22 * L), BF),
            pltpu.VMEM((C3, 24 * L), F32),
            pltpu.VMEM((24, 22 * L), F32),
            pltpu.VMEM((C + 32, 2 * L), F32),
        ],
        "generator",
    )(up, mid, down, w_gen, w_rgb)

    edges = neighbours(far, "frame", 2) + neighbours(near, "frame", 1) + [near]
    grad_in, pack = call(
        disc_kernel,
        (jax.ShapeDtypeStruct((C, 2048), BF), jax.ShapeDtypeStruct((8, 24, 14 * C), BF)),
        [
            pltpu.VMEM((10, C + 32, L), F32),
            pltpu.VMEM((10, 48, 18 * L), BF),
            pltpu.VMEM((10, 16, L), F32),
            pltpu.VMEM((8, C3, 18 * L), BF),
            pltpu.VMEM((6, C3, 16 * L), BF),
            pltpu.VMEM((4, C3, 14 * L), BF),
            pltpu.VMEM((16, 12 * L), BF),
            pltpu.VMEM((C3, 10 * L), BF),
            pltpu.VMEM((C3, 18 * L), F32),
            pltpu.VMEM((2 * C, 18 * L), F32),
            pltpu.VMEM((24, 14 * L), F32),
            pltpu.VMEM((C3, 12 * C), F32),
            pltpu.VMEM((144, C), F32),
            pltpu.VMEM((32, C3), F32),
            pltpu.VMEM((C, L), F32),
        ],
        "discriminator",
    )(
        *edges,
        w_one, w_two, w_two_back, w_one_back, w_rgb_back, w_gen_back, score_w, hid, gen_pad,
    )

    gen_one, gen_rgb, disc_one, disc_two, disc_score = call(
        functools.partial(finish_kernel, factor),
        (
            jax.ShapeDtypeStruct((9, C * C), F32),
            jax.ShapeDtypeStruct((3, 3, 3, C), F32),
            jax.ShapeDtypeStruct((3, 3, 3, 3, C), F32),
            jax.ShapeDtypeStruct((27, C * C), F32),
            jax.ShapeDtypeStruct((1, C), F32),
        ),
        [
            pltpu.VMEM((7, C3, L), F32),
            pltpu.VMEM((36 * 32, L), F32),
        ],
        "finish",
    )(*summed(pack))
    gen_rgb = jnp.transpose(gen_rgb, (0, 3, 1, 2))
    disc_one = jnp.transpose(disc_one, (4, 0, 1, 2, 3))
    return (grad_in.reshape(gen_in.shape), gen_one, gen_rgb, disc_one, disc_two, disc_score.reshape(C))


def solution(mesh):
    in_specs = (
        P(None, "frame", "section", None),
        P(),
        P(),
        P(),
        P(),
        P(),
        P("frame", "section", None),
    )
    out_specs = (P(None, "frame", "section", None), P(), P(), P(), P(), P())
    return jax.shard_map(local, mesh=mesh, in_specs=in_specs, out_specs=out_specs, check_vma=False)
```

```python
import functools

import jax
import jax.numpy as jnp
from jax import lax
from jax.experimental import pallas as pl
from jax.experimental.pallas import tpu as pltpu
from jax.sharding import PartitionSpec as P

BF = jnp.bfloat16
F32 = jnp.float32
C = 64
C3 = 3 * C
L = 128
BOTH = ("section", "frame")


def span(row, rows=1):
    return slice(row * L, (row + rows) * L)


def lanes():
    return lax.broadcasted_iota(jnp.int32, (1, L), 1)


def sides(value):
    at = lanes()
    left = jnp.where(at == 0, 0.0, pltpu.roll(value, 1, 1))
    right = jnp.where(at == L - 1, 0.0, pltpu.roll(value, L - 1, 1))
    return left, right


def put(ref, row, value):
    left, right = sides(value)
    ref[0:C, span(row)] = left.astype(BF)
    ref[C : 2 * C, span(row)] = value.astype(BF)
    ref[2 * C : C3, span(row)] = right.astype(BF)


def inside(index, size):
    return jnp.where(jnp.logical_and(index >= 0, index < size), 1.0, 0.0).astype(F32)


def staged(out, weight, block, rows, outs, lag, finish, step=2):
    done = 0
    for row in range(0, rows, step):
        part = span(row, min(step, rows - row))
        out[:, part] = jnp.dot(weight[...], block(part), preferred_element_type=F32)
        while done < min(row - lag, outs):
            finish(done)
            done += 1
    for row in range(done, outs):
        finish(row)


def tap_rows(part, row, outs, first=0, pitch=None):
    pitch = pitch or outs
    return (
        part[first : first + outs, span(row)]
        + part[first + pitch : first + pitch + outs, span(row + 1)]
        + part[first + 2 * pitch : first + 2 * pitch + outs, span(row + 2)]
    )


def along_lanes(a, b):
    return lax.dot_general(a, b, (((1,), (1,)), ((), ())), preferred_element_type=F32)


def three_rows(value):
    blank = jnp.zeros((value.shape[0], L), BF)
    return jnp.concatenate(
        [
            jnp.concatenate([value, blank, blank], axis=1),
            jnp.concatenate([blank, value, blank], axis=1),
            jnp.concatenate([blank, blank, value], axis=1),
        ],
        axis=0,
    )


def pack_kernel(features, scores, mid, wide):
    wide[...] = features[...].astype(F32)
    sub = lax.broadcasted_iota(jnp.int32, (16, L), 0)
    for k in range(16):
        mid[0:C, span(k)] = wide[pl.ds(k, C, stride=16), :].astype(BF)
        score = scores[k : k + 1, :]
        high = score.astype(BF).astype(F32)
        both = jnp.where(sub == 0, high, jnp.where(sub == 1, score - high, 0.0))
        mid[C : C + 16, span(k)] = both.astype(BF)


def weight_kernel(
    flat_two, flat_gen, two, two_back, gen, gen_back, taps, blocks,
):
    for j in range(32):
        taps[pl.ds(j, 27, stride=32), :] = flat_two[:, span(j)].astype(F32)
        taps[pl.ds(27 * 32 + j, 9, stride=32), :] = flat_gen[:, span(j)].astype(F32)
    for dr in range(3):
        for b in range(6):
            pair = []
            for tap in (2 * b, 2 * b + 1):
                at = (tap // 3) * 9 + dr * 3 + tap % 3 if tap < 9 else 27 + dr * 3 + tap - 9
                pair.append(taps[32 * at : 32 * at + 32, :])
            for odd in range(2):
                half = slice(C * odd, C * odd + C)
                blocks[b, pl.ds(C * dr + odd, 32, stride=2), :] = jnp.concatenate(
                    [pair[0][:, half], pair[1][:, half]], axis=1
                )
    for dr in range(3):
        rows = slice(C * dr, C * dr + C)
        mirror = slice(C * (2 - dr), C * (2 - dr) + C)
        ahead = [blocks[b, rows, :] for b in range(6)]
        ahead = [block[:, C * h : C * h + C] for block in ahead for h in range(2)]
        two[rows, :] = jnp.concatenate(ahead[:9], axis=1).astype(BF)
        gen[rows, :] = jnp.concatenate(ahead[9:], axis=1).astype(BF)
        back = [jnp.transpose(blocks[b, rows, :]) for b in range(6)]
        back = [block[C * h : C * h + C, :] for block in back for h in range(2)]
        two_back[mirror, :] = jnp.concatenate(back[8::-1], axis=1).astype(BF)
        gen_back[mirror, :] = jnp.concatenate(back[:8:-1], axis=1).astype(BF)


def gen_kernel(up, mid, down, w_gen, w_rgb, near, far, hid, gen, gs, hs, part, part_rgb, rows):
    section = lax.axis_index("section")
    rows_all = 8 * lax.axis_size("section")
    base = section * 8

    rows[...] = jnp.zeros_like(rows)
    for f in range(2):
        for row in range(24):
            source = (up, mid, down)[row // 8]
            keep = inside(base + row - 8, rows_all)
            value = source[0:C, span(f * 8 + row % 8)].astype(F32) * keep
            put(gs, row, value)
        def hidden_row(row):
            keep = inside(base + row - 7, rows_all)
            put(hs, row, jnp.tanh(tap_rows(part, row, C)) * keep)

        def colour_row(row):
            keep = inside(base + row - 6, rows_all)
            rows[3 * row : 3 * row + 3, span(f)] = (tap_rows(part_rgb, row, 8) * keep)[0:3]

        staged(part, w_gen, lambda s: gs[:, s], 24, 22, 2, hidden_row)
        gen[f] = gs[:, span(7, 10)]
        staged(part_rgb, w_rgb, lambda s: hs[:, s], 22, 20, 2, colour_row)
        hid[f] = hs[:, span(6, 10)]
        for row in range(16):
            at = row + 4
            source = (up, mid, down)[at // 8]
            keep = inside(base + row - 4, rows_all)
            score = source[C : C + 16, span(f * 8 + at % 8)].astype(F32) * keep
            rows[C + row : C + row + 1, span(f)] = score[0:1]
            rows[C + 16 + row : C + 17 + row, span(f)] = score[1:2]
    near[...] = rows[...].astype(BF)
    far[...] = rows[0:C, :].astype(BF)


def disc_kernel(
    far_a, far_b, near_a, near_b, home, w_one, w_two, w_two_back, w_one_back, w_rgb_back, w_gen_back, w_score, hid, gen,
    grad_in, pack,
    es, cs, sg, fs, ds, zs, dcs, hzs, wide, wide_back, part, part_two, part_one, part_col, acc, acc_one, acc_rgb, acc_score,
):
    section = lax.axis_index("section")
    frame = lax.axis_index("frame")
    rows_all = 8 * lax.axis_size("section")
    frames_all = 2 * lax.axis_size("frame")
    base = section * 8
    first = frame * 2
    sub = lax.broadcasted_iota(jnp.int32, (8, L), 0)

    blank = jnp.zeros((C, C3), BF)
    for once, twice in ((w_two, wide), (w_two_back, wide_back)):
        for dr in range(3):
            rows = once[C * dr : C * dr + C, :]
            at = 2 * C * dr
            twice[at : at + C, :] = jnp.concatenate([rows, blank], axis=1)
            twice[at + C : at + 2 * C, :] = jnp.concatenate([blank, rows], axis=1)

    turn_far, turn_near = (frame >> 1) & 1, frame & 1
    blocks = (
        (far_a, jnp.where(turn_far == 0, 8, 0), C),
        (far_b, jnp.where(turn_far == 0, 0, 8), C),
        (near_a, jnp.where(turn_near == 0, 6, 2), C + 32),
        (near_b, jnp.where(turn_near == 0, 2, 6), C + 32),
        (home, 4, C + 32),
    )
    es[...] = jnp.zeros_like(es)
    for block, at, size in blocks:
        for j in range(2):
            es[at + j, 0:size, :] = block[:, span(j)].astype(F32)

    def colour_step(e, carry):
        keep = inside(first + e - 4, frames_all)
        sg[e] = (es[e, C : C + 16, :] + es[e, C + 16 : C + 32, :]) * keep
        for row in range(20):
            value = jnp.where(sub < 3, es[e, 3 * row : 3 * row + 8, :] * keep, 0.0)
            left, right = sides(value)
            block = jnp.concatenate([left + pltpu.roll(value, 4, 0), right], axis=0).astype(BF)
            for dr in range(3):
                if 0 <= row - dr < 18:
                    cs[e, dr * 16 : (dr + 1) * 16, span(row - dr)] = block
        return carry

    lax.fori_loop(0, 10, colour_step, 0)

    def feat_step(p, carry):
        def feat_row(row):
            keep_row = inside(base + row - 5, rows_all)
            for j in range(2):
                keep = keep_row * inside(first + 2 * p + j - 3, frames_all)
                put(fs.at[2 * p + j], row, jnp.tanh(part_one[j * C : (j + 1) * C, span(row)]) * keep)

        staged(part_one, w_one, lambda s: cs[pl.ds(2 * p, 4), :, s].reshape(192, -1), 18, 18, 0, feat_row)
        return carry

    lax.fori_loop(0, 4, feat_step, 0)

    acc_score[...] = jnp.zeros_like(acc_score)

    def score_step(p, carry):
        def score_row(row):
            for j in range(2):
                value = jnp.tanh(tap_rows(part_two, row, C, j * C, 2 * C)).astype(BF).astype(F32)
                score = sg[2 * p + j + 2, row : row + 1, :]
                if 4 <= row < 12:
                    acc_score[...] += value * (score * inside(p - 1, 1))
                put(ds.at[2 * p + j], row, w_score[...] * score * (1.0 - value * value))

        staged(part_two, wide, lambda s: fs[pl.ds(2 * p, 4), :, s].reshape(4 * C3, -1), 18, 16, 2, score_row)
        return carry

    lax.fori_loop(0, 3, score_step, 0)

    def back_step(p, carry):
        def back_row(row):
            keep_row = inside(base + row - 3, rows_all)
            for j in range(2):
                keep = keep_row * inside(first + 2 * p + j - 1, frames_all)
                value = fs[2 * p + j + 2, C : 2 * C, span(row + 2)].astype(F32)
                total = tap_rows(part_two, row, C, j * C, 2 * C)
                put(zs.at[2 * p + j], row, total * ((1.0 - value * value) * keep))

        staged(part_two, wide_back, lambda s: ds[pl.ds(2 * p, 4), :, s].reshape(4 * C3, -1), 16, 14, 2, back_row)
        return carry

    lax.fori_loop(0, 2, back_step, 0)

    for f in range(2):
        feat = fs[f + 2 : f + 5, :, span(4, 10)].reshape(3 * C3, 10 * L)
        grad = along_lanes(three_rows(ds[f + 2, C : 2 * C, span(4, 8)]), feat)
        acc[:, : 3 * C3] = grad if f == 0 else acc[:, : 3 * C3] + grad
        colours = cs[f + 3 : f + 6, :, span(5, 8)].reshape(144, 8 * L)
        grad = along_lanes(colours, zs[f + 1, C : 2 * C, span(3, 8)])
        acc_one[...] = grad if f == 0 else acc_one[...] + grad

        colour_rows = []

        def colour_row(row):
            keep = inside(base + row - 2, rows_all)
            value = (tap_rows(part_col, row, 8) * keep).astype(BF).astype(F32)
            colour_rows.append(value)
            left, right = sides(value)
            block = jnp.concatenate([left + pltpu.roll(value, 4, 0), right], axis=0)
            dcs[:, span(row)] = block.astype(BF)

        staged(part_col, w_one_back, lambda s: zs[f : f + 3, :, s].reshape(3 * C3, -1), 14, 12, 2, colour_row)
        own = jnp.concatenate(colour_rows[2:10], axis=1)
        blank = jnp.zeros((8, L), F32)
        own3 = jnp.concatenate(
            [
                jnp.concatenate([own, blank, blank], axis=1),
                jnp.concatenate([blank, own, blank], axis=1),
                jnp.concatenate([blank, blank, own], axis=1),
                jnp.zeros((8, 10 * L), F32),
            ],
            axis=0,
        ).astype(BF)
        grad = along_lanes(own3, hid[f])
        acc_rgb[...] = grad if f == 0 else acc_rgb[...] + grad

        def hidden_row(row):
            keep = inside(base + row - 1, rows_all)
            value = hid[f, C : 2 * C, span(row)].astype(F32)
            put(hzs, row, tap_rows(part, row, C) * ((1.0 - value * value) * keep))

        def input_row(row):
            grad_in[:, span(f * 8 + row)] = tap_rows(part, row, C).astype(BF)

        staged(part, w_rgb_back, lambda s: dcs[:, s], 12, 10, 2, hidden_row)
        grad = along_lanes(three_rows(hzs[C : 2 * C, span(1, 8)]), gen[f])
        acc[:, 3 * C3 :] = grad if f == 0 else acc[:, 3 * C3 :] + grad
        staged(part, w_gen_back, lambda s: hzs[:, s], 10, 8, 2, input_row)

    score = jnp.sum(jnp.transpose(acc_score[...]), axis=0, keepdims=True)
    ones = jnp.concatenate([acc_one[...], jnp.zeros((C3 - 144, C), F32)], axis=0)
    colours = [acc_rgb[0:24, C * k : C * k + C] for k in range(3)]
    colours = jnp.concatenate(colours + [score, jnp.zeros((C3 - 73, C), F32)], axis=0)
    tail = jnp.concatenate([ones, colours], axis=1)
    for k in range(8):
        block = [acc[C * dr + 8 * k : C * dr + 8 * k + 8, :] for dr in range(3)]
        whole = jnp.concatenate([jnp.concatenate(block, axis=0), tail[24 * k : 24 * k + 24]], axis=1)
        pack[k] = whole.astype(BF)


def finish_kernel(factor, own, three, two, one, other, gen_one, gen_rgb, disc_one, disc_two, disc_score, total, taps):
    section = lax.axis_index("section")
    core, y = section & 1, (section >> 2) & 3
    for at, (k, block) in enumerate(((0, own), (3, three), (2, two), (1, one))):
        rows = pl.ds(pl.multiple_of((core * 4 + (y ^ k)) * 24, 8), 24)
        others = pl.ds(pl.multiple_of(((1 - core) * 4 + (y ^ k)) * 24, 8), 24)
        for b in range(7):
            total[b, rows, :] = block[:, span(b)].astype(F32) * factor
            total[b, others, :] = other[at, :, span(b)].astype(F32) * factor
    for c in range(3):
        for dr in range(3):
            for df in range(3):
                disc_one[c, df, dr] = total[6, pl.ds(48 * df + 16 * dr + c, 3, stride=4), :][:, 0:C]
            for dw in range(3):
                at = 24 * dw + 8 * dr + c
                gen_rgb[c, dr, dw : dw + 1, :] = total[6, at : at + 1, :][:, C:]
    disc_score[...] = total[6, 72:73, :][:, C:]
    for dr in range(3):
        for b in range(6):
            for pair in range(4):
                first, second = (
                    total[b, pl.ds(8 * dr + 2 * pair + odd, 8, stride=24), :] for odd in range(2)
                )
                for h in range(2):
                    half = slice(C * h, C * h + C)
                    tap = 2 * b + h
                    at = (tap // 3) * 9 + dr * 3 + tap % 3 if tap < 9 else 27 + dr * 3 + tap - 9
                    taps[pl.ds(32 * at + pair, 8, stride=4), :] = jnp.concatenate(
                        [first[:, half], second[:, half]], axis=1
                    )
    for j in range(32):
        disc_two[:, span(j)] = taps[pl.ds(j, 27, stride=32), :]
        gen_one[:, span(j)] = taps[pl.ds(27 * 32 + j, 9, stride=32), :]


def call(kernel, outs, scratch, name):
    return pl.pallas_call(
        kernel,
        out_shape=outs,
        scratch_shapes=scratch,
        compiler_params=pltpu.CompilerParams(vmem_limit_bytes=52 << 20),
        name=name,
    )


def cyclic(value, axis, step):
    size = lax.axis_size(axis)
    return lax.ppermute(value, axis, [(i, (i + step) % size) for i in range(size)])


def swapped(value, axis, mask):
    return lax.ppermute(value, axis, [(i, i ^ mask) for i in range(lax.axis_size(axis))])


def neighbours(value, axis, step):
    size = lax.axis_size(axis)
    found = []
    for turn in range(2):
        pairs = [(i, (i + step) % size) for i in range(size) if (i // step) % 2 == turn]
        found.append(lax.ppermute(value, axis, pairs + [(j, i) for i, j in pairs]))
    return found


def pick(value, at):
    return lax.dynamic_index_in_dim(value, at, 0, keepdims=False)


def plus(values):
    total = values[0].astype(F32)
    for value in values[1:]:
        total = total + value.astype(F32)
    return total.astype(BF)


def all_sum4(value, axis, low):
    three, two, one = (swapped(value, axis, m * low).astype(F32) for m in (3, 2, 1))
    return ((three + two) + (one + value.astype(F32))).astype(BF)


def summed(value):
    section = lax.axis_index("section")
    core, y = section & 1, (section >> 2) & 3
    halves = value.reshape((2, 4) + value.shape[1:])
    mine = plus([pick(halves, core), swapped(pick(halves, 1 - core), "section", 1)])
    own = plus([pick(mine, y)] + [swapped(pick(mine, y ^ m), "section", 4 * m) for m in (1, 3, 2)])
    own = all_sum4(own, "frame", 4)
    own = plus([own, swapped(own, "section", 2)])
    own = all_sum4(own, "frame", 1)
    three, two, one = (swapped(own, "section", 4 * m) for m in (3, 2, 1))
    blocks = [own, three, two, one]
    return blocks + [swapped(jnp.stack(blocks), "section", 1)]


def local(gen_in, w_gen_one, w_gen_rgb, w_disc_one, w_disc_two, w_score, score_grad):
    cells = 2048 * lax.axis_size("frame") * lax.axis_size("section")
    factor = 1.0 / cells**0.5

    rgb = jnp.pad(jnp.transpose(w_gen_rgb, (2, 0, 3, 1)), ((0, 0), (0, 5), (0, 0), (0, 0)))
    w_rgb = rgb.reshape(24, C3)
    rgb_back = jnp.transpose(jnp.flip(w_gen_rgb, (2, 3)), (2, 1, 3, 0))
    w_rgb_back = jnp.pad(rgb_back, ((0, 0), (0, 0), (0, 1), (0, 1))).reshape(C3, 16)
    one = jnp.transpose(w_disc_one, (0, 2, 3, 4, 1))
    one = jnp.pad(one, ((0, 0), (0, 0), (0, 0), (0, 1), (0, 1))).reshape(C, 144)
    w_one = jnp.concatenate(
        [jnp.pad(one, ((0, 0), (0, 48))), jnp.pad(one, ((0, 0), (48, 0)))], axis=0
    )
    one_back = jnp.transpose(jnp.flip(w_disc_one, (2, 3, 4)), (3, 1, 2, 4, 0))
    w_one_back = jnp.pad(one_back, ((0, 0), (0, 5), (0, 0), (0, 0), (0, 0))).reshape(24, 3 * C3)
    w_two, w_two_back, w_gen, w_gen_back = call(
        weight_kernel,
        (
            jax.ShapeDtypeStruct((C3, 3 * C3), BF),
            jax.ShapeDtypeStruct((C3, 3 * C3), BF),
            jax.ShapeDtypeStruct((C3, C3), BF),
            jax.ShapeDtypeStruct((C3, C3), BF),
        ),
        [pltpu.VMEM((36 * 32, L), F32), pltpu.VMEM((6, C3, L), F32)],
        "weights",
    )(w_disc_two, w_gen_one)

    mid = call(
        pack_kernel,
        jax.ShapeDtypeStruct((C + 16, 2048), BF),
        [pltpu.VMEM((16 * C, L), F32)],
        "pack",
    )(gen_in.reshape(16 * C, L), score_grad.reshape(16, L))
    up = cyclic(mid, "section", 1)
    down = cyclic(mid, "section", -1)

    score_w = jnp.broadcast_to(w_score.astype(F32)[:, None], (C, L))
    w_rgb, w_one, w_one_back, w_rgb_back, score_w = lax.optimization_barrier(
        (w_rgb, w_one, w_one_back, w_rgb_back, score_w)
    )
    near, far, hid, gen_pad = call(
        gen_kernel,
        (
            jax.ShapeDtypeStruct((C + 32, 2 * L), BF),
            jax.ShapeDtypeStruct((C, 2 * L), BF),
            jax.ShapeDtypeStruct((2, C3, 10 * L), BF),
            jax.ShapeDtypeStruct((2, C3, 10 * L), BF),
        ),
        [
            pltpu.VMEM((C3, 24 * L), BF),
            pltpu.VMEM((C3, 22 * L), BF),
            pltpu.VMEM((C3, 24 * L), F32),
            pltpu.VMEM((24, 22 * L), F32),
            pltpu.VMEM((C + 32, 2 * L), F32),
        ],
        "generator",
    )(up, mid, down, w_gen, w_rgb)

    edges = neighbours(far, "frame", 2) + neighbours(near, "frame", 1) + [near]
    grad_in, pack = call(
        disc_kernel,
        (jax.ShapeDtypeStruct((C, 2048), BF), jax.ShapeDtypeStruct((8, 24, 14 * C), BF)),
        [
            pltpu.VMEM((10, C + 32, L), F32),
            pltpu.VMEM((10, 48, 18 * L), BF),
            pltpu.VMEM((10, 16, L), F32),
            pltpu.VMEM((8, C3, 18 * L), BF),
            pltpu.VMEM((6, C3, 16 * L), BF),
            pltpu.VMEM((4, C3, 14 * L), BF),
            pltpu.VMEM((16, 12 * L), BF),
            pltpu.VMEM((C3, 10 * L), BF),
            pltpu.VMEM((2 * C3, 4 * C3), BF),
            pltpu.VMEM((2 * C3, 4 * C3), BF),
            pltpu.VMEM((C3, 18 * L), F32),
            pltpu.VMEM((2 * C3, 18 * L), F32),
            pltpu.VMEM((2 * C, 18 * L), F32),
            pltpu.VMEM((24, 14 * L), F32),
            pltpu.VMEM((C3, 12 * C), F32),
            pltpu.VMEM((144, C), F32),
            pltpu.VMEM((32, C3), F32),
            pltpu.VMEM((C, L), F32),
        ],
        "discriminator",
    )(
        *edges,
        w_one, w_two, w_two_back, w_one_back, w_rgb_back, w_gen_back, score_w, hid, gen_pad,
    )

    gen_one, gen_rgb, disc_one, disc_two, disc_score = call(
        functools.partial(finish_kernel, factor),
        (
            jax.ShapeDtypeStruct((9, C * C), F32),
            jax.ShapeDtypeStruct((3, 3, 3, C), F32),
            jax.ShapeDtypeStruct((3, 3, 3, 3, C), F32),
            jax.ShapeDtypeStruct((27, C * C), F32),
            jax.ShapeDtypeStruct((1, C), F32),
        ),
        [
            pltpu.VMEM((7, C3, L), F32),
            pltpu.VMEM((36 * 32, L), F32),
        ],
        "finish",
    )(*summed(pack))
    gen_rgb = jnp.transpose(gen_rgb, (0, 3, 1, 2))
    disc_one = jnp.transpose(disc_one, (4, 0, 1, 2, 3))
    return (grad_in.reshape(gen_in.shape), gen_one, gen_rgb, disc_one, disc_two, disc_score.reshape(C))


def solution(mesh):
    in_specs = (
        P(None, "frame", "section", None),
        P(),
        P(),
        P(),
        P(),
        P(),
        P("frame", "section", None),
    )
    out_specs = (P(None, "frame", "section", None), P(), P(), P(), P(), P())
    return jax.shard_map(local, mesh=mesh, in_specs=in_specs, out_specs=out_specs, check_vma=False)
```

```python
import functools

import jax
import jax.numpy as jnp
from jax import lax
from jax.experimental import pallas as pl
from jax.experimental.pallas import tpu as pltpu
from jax.sharding import PartitionSpec as P

BF = jnp.bfloat16
F32 = jnp.float32
C = 64
C3 = 3 * C
L = 128
BOTH = ("section", "frame")


def span(row, rows=1):
    return slice(row * L, (row + rows) * L)


def lanes():
    return lax.broadcasted_iota(jnp.int32, (1, L), 1)


def sides(value):
    at = lanes()
    left = jnp.where(at == 0, 0.0, pltpu.roll(value, 1, 1))
    right = jnp.where(at == L - 1, 0.0, pltpu.roll(value, L - 1, 1))
    return left, right


def put(ref, row, value):
    left, right = sides(value)
    ref[0:C, span(row)] = left.astype(BF)
    ref[C : 2 * C, span(row)] = value.astype(BF)
    ref[2 * C : C3, span(row)] = right.astype(BF)


def inside(index, size):
    return jnp.where(jnp.logical_and(index >= 0, index < size), 1.0, 0.0).astype(F32)


def staged(out, weight, block, rows, outs, lag, finish, step=2):
    done = 0
    for row in range(0, rows, step):
        part = span(row, min(step, rows - row))
        out[:, part] = jnp.dot(weight[...], block(part), preferred_element_type=F32)
        while done < min(row - lag, outs):
            finish(done)
            done += 1
    for row in range(done, outs):
        finish(row)


def tap_rows(part, row, outs, first=0, pitch=None):
    pitch = pitch or outs
    return (
        part[first : first + outs, span(row)]
        + part[first + pitch : first + pitch + outs, span(row + 1)]
        + part[first + 2 * pitch : first + 2 * pitch + outs, span(row + 2)]
    )


def along_lanes(a, b):
    return lax.dot_general(a, b, (((1,), (1,)), ((), ())), preferred_element_type=F32)


def three_rows(value):
    blank = jnp.zeros((value.shape[0], L), BF)
    return jnp.concatenate(
        [
            jnp.concatenate([value, blank, blank], axis=1),
            jnp.concatenate([blank, value, blank], axis=1),
            jnp.concatenate([blank, blank, value], axis=1),
        ],
        axis=0,
    )


def pack_kernel(features, scores, mid, wide):
    wide[...] = features[...].astype(F32)
    sub = lax.broadcasted_iota(jnp.int32, (16, L), 0)
    for k in range(16):
        mid[0:C, span(k)] = wide[pl.ds(k, C, stride=16), :].astype(BF)
        score = scores[k : k + 1, :]
        high = score.astype(BF).astype(F32)
        both = jnp.where(sub == 0, high, jnp.where(sub == 1, score - high, 0.0))
        mid[C : C + 16, span(k)] = both.astype(BF)


def weight_kernel(
    flat_two, flat_gen, two, two_back, gen, gen_back, taps, blocks,
):
    for j in range(32):
        taps[pl.ds(j, 27, stride=32), :] = flat_two[:, span(j)].astype(F32)
        taps[pl.ds(27 * 32 + j, 9, stride=32), :] = flat_gen[:, span(j)].astype(F32)
    for dr in range(3):
        for b in range(6):
            pair = []
            for tap in (2 * b, 2 * b + 1):
                at = (tap // 3) * 9 + dr * 3 + tap % 3 if tap < 9 else 27 + dr * 3 + tap - 9
                pair.append(taps[32 * at : 32 * at + 32, :])
            for odd in range(2):
                half = slice(C * odd, C * odd + C)
                blocks[b, pl.ds(C * dr + odd, 32, stride=2), :] = jnp.concatenate(
                    [pair[0][:, half], pair[1][:, half]], axis=1
                )
    for dr in range(3):
        rows = slice(C * dr, C * dr + C)
        mirror = slice(C * (2 - dr), C * (2 - dr) + C)
        ahead = [blocks[b, rows, :] for b in range(6)]
        ahead = [block[:, C * h : C * h + C] for block in ahead for h in range(2)]
        once = jnp.concatenate(ahead[:9], axis=1).astype(BF)
        blank = jnp.zeros((C, C3), BF)
        two[2 * C * dr : 2 * C * dr + C, :] = jnp.concatenate([once, blank], axis=1)
        two[2 * C * dr + C : 2 * C * dr + 2 * C, :] = jnp.concatenate([blank, once], axis=1)
        gen[rows, :] = jnp.concatenate(ahead[9:], axis=1).astype(BF)
        back = [jnp.transpose(blocks[b, rows, :]) for b in range(6)]
        back = [block[C * h : C * h + C, :] for block in back for h in range(2)]
        once = jnp.concatenate(back[8::-1], axis=1).astype(BF)
        at = 2 * C * (2 - dr)
        two_back[at : at + C, :] = jnp.concatenate([once, blank], axis=1)
        two_back[at + C : at + 2 * C, :] = jnp.concatenate([blank, once], axis=1)
        gen_back[mirror, :] = jnp.concatenate(back[:8:-1], axis=1).astype(BF)


def gen_kernel(up, mid, down, w_gen, w_rgb, near, far, hid, gen, gs, hs, part, part_rgb, rows):
    section = lax.axis_index("section")
    rows_all = 8 * lax.axis_size("section")
    base = section * 8

    rows[...] = jnp.zeros_like(rows)
    for f in range(2):
        for row in range(24):
            source = (up, mid, down)[row // 8]
            keep = inside(base + row - 8, rows_all)
            value = source[0:C, span(f * 8 + row % 8)].astype(F32) * keep
            put(gs, row, value)
        def hidden_row(row):
            keep = inside(base + row - 7, rows_all)
            put(hs, row, jnp.tanh(tap_rows(part, row, C)) * keep)

        def colour_row(row):
            keep = inside(base + row - 6, rows_all)
            rows[3 * row : 3 * row + 3, span(f)] = (tap_rows(part_rgb, row, 8) * keep)[0:3]

        staged(part, w_gen, lambda s: gs[:, s], 24, 22, 2, hidden_row)
        gen[f] = gs[:, span(7, 10)]
        staged(part_rgb, w_rgb, lambda s: hs[:, s], 22, 20, 2, colour_row)
        hid[f] = hs[:, span(6, 10)]
        for row in range(16):
            at = row + 4
            source = (up, mid, down)[at // 8]
            keep = inside(base + row - 4, rows_all)
            score = source[C : C + 16, span(f * 8 + at % 8)].astype(F32) * keep
            rows[C + row : C + row + 1, span(f)] = score[0:1]
            rows[C + 16 + row : C + 17 + row, span(f)] = score[1:2]
    near[...] = rows[...].astype(BF)
    far[...] = rows[0:C, :].astype(BF)


def disc_kernel(
    far_a, far_b, near_a, near_b, home, w_one, w_two, w_two_back, w_one_back, w_rgb_back, w_gen_back, w_score, hid, gen,
    grad_in, pack,
    es, cs, sg, fs, ds, zs, dcs, hzs, part, part_two, part_one, part_col, acc, acc_one, acc_rgb, acc_score,
):
    section = lax.axis_index("section")
    frame = lax.axis_index("frame")
    rows_all = 8 * lax.axis_size("section")
    frames_all = 2 * lax.axis_size("frame")
    base = section * 8
    first = frame * 2
    sub = lax.broadcasted_iota(jnp.int32, (8, L), 0)

    turn_far, turn_near = (frame >> 1) & 1, frame & 1
    blocks = (
        (far_a, jnp.where(turn_far == 0, 8, 0), C),
        (far_b, jnp.where(turn_far == 0, 0, 8), C),
        (near_a, jnp.where(turn_near == 0, 6, 2), C + 32),
        (near_b, jnp.where(turn_near == 0, 2, 6), C + 32),
        (home, 4, C + 32),
    )
    es[...] = jnp.zeros_like(es)
    for block, at, size in blocks:
        for j in range(2):
            es[at + j, 0:size, :] = block[:, span(j)].astype(F32)

    def colour_step(e, carry):
        keep = inside(first + e - 4, frames_all)
        sg[e] = (es[e, C : C + 16, :] + es[e, C + 16 : C + 32, :]) * keep
        for row in range(20):
            value = jnp.where(sub < 3, es[e, 3 * row : 3 * row + 8, :] * keep, 0.0)
            left, right = sides(value)
            block = jnp.concatenate([left + pltpu.roll(value, 4, 0), right], axis=0).astype(BF)
            for dr in range(3):
                if 0 <= row - dr < 18:
                    cs[e, dr * 16 : (dr + 1) * 16, span(row - dr)] = block
        return carry

    lax.fori_loop(0, 10, colour_step, 0)

    def feat_step(p, carry):
        def feat_row(row):
            keep_row = inside(base + row - 5, rows_all)
            for j in range(2):
                keep = keep_row * inside(first + 2 * p + j - 3, frames_all)
                put(fs.at[2 * p + j], row, jnp.tanh(part_one[j * C : (j + 1) * C, span(row)]) * keep)

        staged(part_one, w_one, lambda s: cs[pl.ds(2 * p, 4), :, s].reshape(192, -1), 18, 18, 0, feat_row)
        return carry

    lax.fori_loop(0, 4, feat_step, 0)

    acc_score[...] = jnp.zeros_like(acc_score)

    def score_step(p, carry):
        def score_row(row):
            for j in range(2):
                value = jnp.tanh(tap_rows(part_two, row, C, j * C, 2 * C)).astype(BF).astype(F32)
                score = sg[2 * p + j + 2, row : row + 1, :]
                if 4 <= row < 12:
                    acc_score[...] += value * (score * inside(p - 1, 1))
                put(ds.at[2 * p + j], row, w_score[...] * score * (1.0 - value * value))

        staged(part_two, w_two, lambda s: fs[pl.ds(2 * p, 4), :, s].reshape(4 * C3, -1), 18, 16, 2, score_row)
        return carry

    lax.fori_loop(0, 3, score_step, 0)

    def back_step(p, carry):
        def back_row(row):
            keep_row = inside(base + row - 3, rows_all)
            for j in range(2):
                keep = keep_row * inside(first + 2 * p + j - 1, frames_all)
                value = fs[2 * p + j + 2, C : 2 * C, span(row + 2)].astype(F32)
                total = tap_rows(part_two, row, C, j * C, 2 * C)
                put(zs.at[2 * p + j], row, total * ((1.0 - value * value) * keep))

        staged(part_two, w_two_back, lambda s: ds[pl.ds(2 * p, 4), :, s].reshape(4 * C3, -1), 16, 14, 2, back_row)
        return carry

    lax.fori_loop(0, 2, back_step, 0)

    for f in range(2):
        feat = fs[f + 2 : f + 5, :, span(4, 10)].reshape(3 * C3, 10 * L)
        grad = along_lanes(three_rows(ds[f + 2, C : 2 * C, span(4, 8)]), feat)
        acc[:, : 3 * C3] = grad if f == 0 else acc[:, : 3 * C3] + grad
        colours = cs[f + 3 : f + 6, :, span(5, 8)].reshape(144, 8 * L)
        grad = along_lanes(colours, zs[f + 1, C : 2 * C, span(3, 8)])
        acc_one[...] = grad if f == 0 else acc_one[...] + grad

        colour_rows = []

        def colour_row(row):
            keep = inside(base + row - 2, rows_all)
            value = (tap_rows(part_col, row, 8) * keep).astype(BF).astype(F32)
            colour_rows.append(value)
            left, right = sides(value)
            block = jnp.concatenate([left + pltpu.roll(value, 4, 0), right], axis=0)
            dcs[:, span(row)] = block.astype(BF)

        staged(part_col, w_one_back, lambda s: zs[f : f + 3, :, s].reshape(3 * C3, -1), 14, 12, 2, colour_row)
        own = jnp.concatenate(colour_rows[2:10], axis=1)
        blank = jnp.zeros((8, L), F32)
        own3 = jnp.concatenate(
            [
                jnp.concatenate([own, blank, blank], axis=1),
                jnp.concatenate([blank, own, blank], axis=1),
                jnp.concatenate([blank, blank, own], axis=1),
                jnp.zeros((8, 10 * L), F32),
            ],
            axis=0,
        ).astype(BF)
        grad = along_lanes(own3, hid[f])
        acc_rgb[...] = grad if f == 0 else acc_rgb[...] + grad

        def hidden_row(row):
            keep = inside(base + row - 1, rows_all)
            value = hid[f, C : 2 * C, span(row)].astype(F32)
            put(hzs, row, tap_rows(part, row, C) * ((1.0 - value * value) * keep))

        def input_row(row):
            grad_in[:, span(f * 8 + row)] = tap_rows(part, row, C).astype(BF)

        staged(part, w_rgb_back, lambda s: dcs[:, s], 12, 10, 2, hidden_row)
        grad = along_lanes(three_rows(hzs[C : 2 * C, span(1, 8)]), gen[f])
        acc[:, 3 * C3 :] = grad if f == 0 else acc[:, 3 * C3 :] + grad
        staged(part, w_gen_back, lambda s: hzs[:, s], 10, 8, 2, input_row)

    score = jnp.sum(jnp.transpose(acc_score[...]), axis=0, keepdims=True)
    ones = jnp.concatenate([acc_one[...], jnp.zeros((C3 - 144, C), F32)], axis=0)
    colours = [acc_rgb[0:24, C * k : C * k + C] for k in range(3)]
    colours = jnp.concatenate(colours + [score, jnp.zeros((C3 - 73, C), F32)], axis=0)
    tail = jnp.concatenate([ones, colours], axis=1)
    for k in range(8):
        block = [acc[C * dr + 8 * k : C * dr + 8 * k + 8, :] for dr in range(3)]
        whole = jnp.concatenate([jnp.concatenate(block, axis=0), tail[24 * k : 24 * k + 24]], axis=1)
        pack[k] = whole.astype(BF)


def finish_kernel(factor, own, three, two, one, other, gen_one, gen_rgb, disc_one, disc_two, disc_score, total, taps):
    section = lax.axis_index("section")
    core, y = section & 1, (section >> 2) & 3
    for at, (k, block) in enumerate(((0, own), (3, three), (2, two), (1, one))):
        rows = pl.ds(pl.multiple_of((core * 4 + (y ^ k)) * 24, 8), 24)
        others = pl.ds(pl.multiple_of(((1 - core) * 4 + (y ^ k)) * 24, 8), 24)
        for b in range(7):
            total[b, rows, :] = block[:, span(b)].astype(F32) * factor
            total[b, others, :] = other[at, :, span(b)].astype(F32) * factor
    for c in range(3):
        for dr in range(3):
            for df in range(3):
                disc_one[c, df, dr] = total[6, pl.ds(48 * df + 16 * dr + c, 3, stride=4), :][:, 0:C]
            for dw in range(3):
                at = 24 * dw + 8 * dr + c
                gen_rgb[c, dr, dw : dw + 1, :] = total[6, at : at + 1, :][:, C:]
    disc_score[...] = total[6, 72:73, :][:, C:]
    for dr in range(3):
        for b in range(6):
            for pair in range(4):
                first, second = (
                    total[b, pl.ds(8 * dr + 2 * pair + odd, 8, stride=24), :] for odd in range(2)
                )
                for h in range(2):
                    half = slice(C * h, C * h + C)
                    tap = 2 * b + h
                    at = (tap // 3) * 9 + dr * 3 + tap % 3 if tap < 9 else 27 + dr * 3 + tap - 9
                    taps[pl.ds(32 * at + pair, 8, stride=4), :] = jnp.concatenate(
                        [first[:, half], second[:, half]], axis=1
                    )
    for j in range(32):
        disc_two[:, span(j)] = taps[pl.ds(j, 27, stride=32), :]
        gen_one[:, span(j)] = taps[pl.ds(27 * 32 + j, 9, stride=32), :]


def call(kernel, outs, scratch, name):
    return pl.pallas_call(
        kernel,
        out_shape=outs,
        scratch_shapes=scratch,
        compiler_params=pltpu.CompilerParams(vmem_limit_bytes=50 << 20),
        name=name,
    )


def cyclic(value, axis, step):
    size = lax.axis_size(axis)
    return lax.ppermute(value, axis, [(i, (i + step) % size) for i in range(size)])


def swapped(value, axis, mask):
    return lax.ppermute(value, axis, [(i, i ^ mask) for i in range(lax.axis_size(axis))])


def neighbours(value, axis, step):
    size = lax.axis_size(axis)
    found = []
    for turn in range(2):
        pairs = [(i, (i + step) % size) for i in range(size) if (i // step) % 2 == turn]
        found.append(lax.ppermute(value, axis, pairs + [(j, i) for i, j in pairs]))
    return found


def pick(value, at):
    return lax.dynamic_index_in_dim(value, at, 0, keepdims=False)


def plus(values):
    total = values[0].astype(F32)
    for value in values[1:]:
        total = total + value.astype(F32)
    return total.astype(BF)


def all_sum4(value, axis, low):
    three, two, one = (swapped(value, axis, m * low).astype(F32) for m in (3, 2, 1))
    return ((three + two) + (one + value.astype(F32))).astype(BF)


def summed(value):
    section = lax.axis_index("section")
    core, y = section & 1, (section >> 2) & 3
    halves = value.reshape((2, 4) + value.shape[1:])
    mine = plus([pick(halves, core), swapped(pick(halves, 1 - core), "section", 1)])
    own = plus([pick(mine, y)] + [swapped(pick(mine, y ^ m), "section", 4 * m) for m in (1, 3, 2)])
    own = all_sum4(own, "frame", 4)
    own = plus([own, swapped(own, "section", 2)])
    own = all_sum4(own, "frame", 1)
    three, two, one = (swapped(own, "section", 4 * m) for m in (3, 2, 1))
    blocks = [own, three, two, one]
    return blocks + [swapped(jnp.stack(blocks), "section", 1)]


def local(gen_in, w_gen_one, w_gen_rgb, w_disc_one, w_disc_two, w_score, score_grad):
    cells = 2048 * lax.axis_size("frame") * lax.axis_size("section")
    factor = 1.0 / cells**0.5

    rgb = jnp.pad(jnp.transpose(w_gen_rgb, (2, 0, 3, 1)), ((0, 0), (0, 5), (0, 0), (0, 0)))
    w_rgb = rgb.reshape(24, C3)
    rgb_back = jnp.transpose(jnp.flip(w_gen_rgb, (2, 3)), (2, 1, 3, 0))
    w_rgb_back = jnp.pad(rgb_back, ((0, 0), (0, 0), (0, 1), (0, 1))).reshape(C3, 16)
    one = jnp.transpose(w_disc_one, (0, 2, 3, 4, 1))
    one = jnp.pad(one, ((0, 0), (0, 0), (0, 0), (0, 1), (0, 1))).reshape(C, 144)
    w_one = jnp.concatenate(
        [jnp.pad(one, ((0, 0), (0, 48))), jnp.pad(one, ((0, 0), (48, 0)))], axis=0
    )
    one_back = jnp.transpose(jnp.flip(w_disc_one, (2, 3, 4)), (3, 1, 2, 4, 0))
    w_one_back = jnp.pad(one_back, ((0, 0), (0, 5), (0, 0), (0, 0), (0, 0))).reshape(24, 3 * C3)
    w_two, w_two_back, w_gen, w_gen_back = call(
        weight_kernel,
        (
            jax.ShapeDtypeStruct((2 * C3, 4 * C3), BF),
            jax.ShapeDtypeStruct((2 * C3, 4 * C3), BF),
            jax.ShapeDtypeStruct((C3, C3), BF),
            jax.ShapeDtypeStruct((C3, C3), BF),
        ),
        [pltpu.VMEM((36 * 32, L), F32), pltpu.VMEM((6, C3, L), F32)],
        "weights",
    )(w_disc_two, w_gen_one)

    mid = call(
        pack_kernel,
        jax.ShapeDtypeStruct((C + 16, 2048), BF),
        [pltpu.VMEM((16 * C, L), F32)],
        "pack",
    )(gen_in.reshape(16 * C, L), score_grad.reshape(16, L))
    up = cyclic(mid, "section", 1)
    down = cyclic(mid, "section", -1)

    score_w = jnp.broadcast_to(w_score.astype(F32)[:, None], (C, L))
    w_rgb, w_one, w_one_back, w_rgb_back, score_w = lax.optimization_barrier(
        (w_rgb, w_one, w_one_back, w_rgb_back, score_w)
    )
    near, far, hid, gen_pad = call(
        gen_kernel,
        (
            jax.ShapeDtypeStruct((C + 32, 2 * L), BF),
            jax.ShapeDtypeStruct((C, 2 * L), BF),
            jax.ShapeDtypeStruct((2, C3, 10 * L), BF),
            jax.ShapeDtypeStruct((2, C3, 10 * L), BF),
        ),
        [
            pltpu.VMEM((C3, 24 * L), BF),
            pltpu.VMEM((C3, 22 * L), BF),
            pltpu.VMEM((C3, 24 * L), F32),
            pltpu.VMEM((24, 22 * L), F32),
            pltpu.VMEM((C + 32, 2 * L), F32),
        ],
        "generator",
    )(up, mid, down, w_gen, w_rgb)

    edges = neighbours(far, "frame", 2) + neighbours(near, "frame", 1) + [near]
    grad_in, pack = call(
        disc_kernel,
        (jax.ShapeDtypeStruct((C, 2048), BF), jax.ShapeDtypeStruct((8, 24, 14 * C), BF)),
        [
            pltpu.VMEM((10, C + 32, L), F32),
            pltpu.VMEM((10, 48, 18 * L), BF),
            pltpu.VMEM((10, 16, L), F32),
            pltpu.VMEM((8, C3, 18 * L), BF),
            pltpu.VMEM((6, C3, 16 * L), BF),
            pltpu.VMEM((4, C3, 14 * L), BF),
            pltpu.VMEM((16, 12 * L), BF),
            pltpu.VMEM((C3, 10 * L), BF),
            pltpu.VMEM((C3, 18 * L), F32),
            pltpu.VMEM((2 * C3, 18 * L), F32),
            pltpu.VMEM((2 * C, 18 * L), F32),
            pltpu.VMEM((24, 14 * L), F32),
            pltpu.VMEM((C3, 12 * C), F32),
            pltpu.VMEM((144, C), F32),
            pltpu.VMEM((32, C3), F32),
            pltpu.VMEM((C, L), F32),
        ],
        "discriminator",
    )(
        *edges,
        w_one, w_two, w_two_back, w_one_back, w_rgb_back, w_gen_back, score_w, hid, gen_pad,
    )

    gen_one, gen_rgb, disc_one, disc_two, disc_score = call(
        functools.partial(finish_kernel, factor),
        (
            jax.ShapeDtypeStruct((9, C * C), F32),
            jax.ShapeDtypeStruct((3, 3, 3, C), F32),
            jax.ShapeDtypeStruct((3, 3, 3, 3, C), F32),
            jax.ShapeDtypeStruct((27, C * C), F32),
            jax.ShapeDtypeStruct((1, C), F32),
        ),
        [
            pltpu.VMEM((7, C3, L), F32),
            pltpu.VMEM((36 * 32, L), F32),
        ],
        "finish",
    )(*summed(pack))
    gen_rgb = jnp.transpose(gen_rgb, (0, 3, 1, 2))
    disc_one = jnp.transpose(disc_one, (4, 0, 1, 2, 3))
    return (grad_in.reshape(gen_in.shape), gen_one, gen_rgb, disc_one, disc_two, disc_score.reshape(C))


def solution(mesh):
    in_specs = (
        P(None, "frame", "section", None),
        P(),
        P(),
        P(),
        P(),
        P(),
        P("frame", "section", None),
    )
    out_specs = (P(None, "frame", "section", None), P(), P(), P(), P(), P())
    return jax.shard_map(local, mesh=mesh, in_specs=in_specs, out_specs=out_specs, check_vma=False)
```
